32 devices in a mesh: rows: 2 (over y), cols: 4 (over z), layers: 4 (over x, core).
Axes of the slice: x: 2, y: 2, z: 4, core: 2. Of those that a mesh axis runs over, the one named last changes fastest.
Arguments:
- y_blocks: bfloat16 [96, 16, 128, 128], P('rows', ('cols', 'layers')), may hold values from -1 to 1
- y_cols: int32 [96, 16], P('rows', ('cols', 'layers')), may hold values from 0 to 95, as said below
- prod_blocks: bfloat16 [96, 16, 128, 128], P('rows', ('cols', 'layers')), may hold values from -1 to 1
- prod_cols: int32 [96, 16], P('rows', ('cols', 'layers')), may hold values from 0 to 95, as said below
- out_cols: int32 [96, 16, 2], P('rows', ('cols', 'layers')), may hold values from 0 to 95, as said below
Outputs:
- y_next: bfloat16 [96, 16, 2, 128, 128], P('rows', ('cols', 'layers'))
The draws below stay inside these ranges and needn't reach their ends.
Inputs may be any that keep to these rules, and one draw needn't show every extreme that they name: y_cols[i, t] lies in [t * 6, (t + 1) * 6): each block row of Y holds exactly one block in each range of 6 block columns. prod_cols[k, t] lies in [t * 6, (t + 1) * 6): each block row of M holds exactly one block in each range of 6 block columns. out_cols[i, t, :] are 2 distinct block columns in [t * 6, (t + 1) * 6), one of them equal to y_cols[i, t].
All inputs are finite; a program needn't handle non-finite values.
Results may differ from the reference program's by a relative error of at most 0.001.
Values may be sent and summed in bfloat16 or wider, within the bound.
A program may use at most 128 MiB of HBM per device.

```python
import jax
import jax.numpy as jnp
from jax import lax

BS = 128
TILE_COLS = 6
OUT_PER_TILE = 2
TILES = 16
NB = 96


def column_offsets(key):
    return jax.random.randint(jax.random.fold_in(key, 11), (NB, TILES), 0, TILE_COLS, dtype=jnp.int32)


def tile_starts():
    return (jnp.arange(TILES, dtype=jnp.int32) * TILE_COLS)[None, :]


def draw_y_cols(key, part):
    return tile_starts() + column_offsets(key)


def draw_prod_cols(key, part):
    offsets = jax.random.randint(jax.random.fold_in(key, 23), (NB, TILES), 0, TILE_COLS, dtype=jnp.int32)
    return tile_starts() + offsets


def draw_out_cols(key, part):
    y_offsets = column_offsets(key)
    candidates = jnp.arange(TILE_COLS, dtype=jnp.int32)
    scores = jax.random.randint(jax.random.fold_in(key, 37), (NB, TILES, TILE_COLS), 0, 1 << 20, dtype=jnp.int32)
    scores = scores * TILE_COLS + candidates[None, None, :]
    scores = jnp.where(candidates[None, None, :] == y_offsets[:, :, None], -1, scores)
    chosen = jnp.argsort(scores, axis=-1, stable=True)[:, :, :OUT_PER_TILE].astype(jnp.int32)
    rotation = jax.random.randint(jax.random.fold_in(key, 41), (NB, TILES, 1), 0, OUT_PER_TILE, dtype=jnp.int32)
    positions = (jnp.arange(OUT_PER_TILE, dtype=jnp.int32)[None, None, :] + rotation) % OUT_PER_TILE
    chosen = jnp.take_along_axis(chosen, positions, axis=-1)
    return tile_starts()[:, :, None] + chosen


def level_of(stream_key, shape, cuts, least, high):
    def one(axis_at, parts):
        draws = jax.random.uniform(jax.random.fold_in(jax.random.fold_in(stream_key, 6), axis_at), (parts,), jnp.float32, least / len(cuts), high / len(cuts))
        return jnp.repeat(jnp.exp(draws), shape[axis_at] // parts).reshape((-1,) + (1,) * (len(shape) - axis_at - 1))

    loudness = one(*cuts[0])
    for cut in cuts[1:]:
        loudness = loudness * one(*cut)
    return loudness


def noise(key, dims, scale, most, pieces=(), held_as=jnp.bfloat16):
    entries = jax.random.normal(key, dims, jnp.float32) * scale
    if len(pieces) > 0:
        entries = level_of(key, dims, pieces, -0.22, 0.18) * entries
    return jnp.clip(entries, min=-most, max=most).astype(held_as)


def setup_inputs(seed: int = 0) -> dict:
    keys = jax.random.split(jax.random.key(seed), 6)
    y_blocks = noise(keys[0], (NB, TILES, BS, BS), 0.18, 1.0, ((0, 2), (1, 16)))
    y_cols = draw_y_cols(jax.random.fold_in(keys[5], 71), 0)
    prod_blocks = noise(keys[2], (NB, TILES, BS, BS), 0.18, 1.0, ((0, 2), (1, 16)))
    prod_cols = draw_prod_cols(jax.random.fold_in(keys[5], 71), 0)
    out_cols = draw_out_cols(jax.random.fold_in(keys[5], 71), 0)
    return dict(y_blocks=y_blocks, y_cols=y_cols, prod_blocks=prod_blocks, prod_cols=prod_cols, out_cols=out_cols)


def reference(y_blocks, y_cols, prod_blocks, prod_cols, out_cols):
    def one_row(block_row):
        left_blocks = y_blocks[block_row].astype(jnp.float32)
        inner_cols = y_cols[block_row]
        right_blocks = prod_blocks[inner_cols].astype(jnp.float32)
        right_cols = prod_cols[inner_cols]
        target_cols = out_cols[block_row]
        present = (right_cols[:, :, None] == target_cols[None, :, :]).astype(jnp.float32)
        products = jnp.einsum("mab,mtbc->mtac", left_blocks, right_blocks)
        summed = jnp.einsum("mtw,mtac->twac", present, products)
        matches = (y_cols[block_row][:, None] == target_cols).astype(jnp.float32)
        updated = 1.5 * matches[:, :, None, None] * left_blocks[:, None] - 0.5 * summed
        return updated.astype(jnp.bfloat16)

    return lax.map(one_row, jnp.arange(NB, dtype=jnp.int32))
```

```python
import functools

import jax
import jax.numpy as jnp
from jax import lax
from jax.experimental import pallas as pl
from jax.experimental.pallas import tpu as pltpu
from jax.sharding import PartitionSpec as P

TILE_COLS = 6
LANES = 128
MESH = pl.DeviceIdType.MESH
UP, DOWN, CROSS, SIBLING = range(4)


def kernel(
    row_count, col_count, y_ref, m_ref, ymeta_ref, pmeta_ref, ycols_ref, out_cols_ref, out_ref,
    yall, mall, acc, ymeta, pmeta, ytable, ptable,
    send_sem, recv_sem, msend_sem, mrecv_sem, row_send, row_recv, rmeta_send, rmeta_recv, local_sem,
):
    rows = y_ref.shape[0]
    half = rows // 2
    r, z, l = lax.axis_index("rows"), lax.axis_index("cols"), lax.axis_index("layers")
    cross = lax.rem(l + 2, 4)
    sibling = l + 1 - 2 * lax.rem(l, 2)
    cross_sibling = lax.rem(sibling + 2, 4)
    paired = z + 1 - 2 * lax.rem(z, 2)
    targets = {UP: (r, z + 1, l), DOWN: (r, z - 1, l), CROSS: (r, z, cross), SIBLING: (r, z, sibling)}

    own_copies = [
        pltpu.make_async_copy(y_ref, yall.at[z, l], local_sem.at[0]),
        pltpu.make_async_copy(m_ref, mall.at[pl.ds(r * rows, rows)], local_sem.at[1]),
        pltpu.make_async_copy(ymeta_ref, ymeta.at[z, l], local_sem.at[2]),
        pltpu.make_async_copy(pmeta_ref, pmeta.at[r], local_sem.at[3]),
    ]
    for copy in own_copies:
        copy.start()

    barrier = pltpu.get_barrier_semaphore()

    def greet(device):
        pl.semaphore_signal(barrier, inc=1, device_id=device, device_id_type=MESH)

    greet(targets[CROSS])
    greet(targets[SIBLING])
    for step in range(1, row_count):
        greet((lax.rem(r + step, row_count), z, l))

    @pl.when(z + 1 < col_count)
    def _():
        greet(targets[UP])

    @pl.when(z > 0)
    def _():
        greet(targets[DOWN])

    line_peers = jnp.where(z > 0, 1, 0) + jnp.where(z + 1 < col_count, 1, 0)
    pl.semaphore_wait(barrier, 1 + row_count + line_peers)

    for copy in own_copies:
        copy.wait()

    def chunk_copy(way, at, tile, part, device):
        return pltpu.make_async_remote_copy(
            src_ref=yall.at[at, tile, pl.ds(part * half, half)],
            dst_ref=yall.at[at, tile, pl.ds(part * half, half)],
            send_sem=send_sem.at[way, at, tile, part],
            recv_sem=recv_sem.at[at, tile, part],
            device_id=device,
            device_id_type=MESH,
        )

    def meta_copy(way, at, tile, device):
        return pltpu.make_async_remote_copy(
            src_ref=ymeta.at[at, tile],
            dst_ref=ymeta.at[at, tile],
            send_sem=msend_sem.at[way, at, tile],
            recv_sem=mrecv_sem.at[at, tile],
            device_id=device,
            device_id_type=MESH,
        )

    def send(way, at, tile, part, start, device=None):
        device = targets[way] if device is None else device
        chunk = chunk_copy(way, at, tile, part, device)
        if start:
            chunk.start()
        else:
            chunk.wait_send()

        @pl.when(part == 0)
        def _():
            meta = meta_copy(way, at, tile, device)
            if start:
                meta.start()
            else:
                meta.wait_send()

    def arrive(at, tile, part):
        chunk_copy(SIBLING, at, tile, part, targets[SIBLING]).wait_recv()

        @pl.when(part == 0)
        def _():
            meta_copy(SIBLING, at, tile, targets[SIBLING]).wait_recv()

    def origins(step):
        away, part = step // 2, lax.rem(step, 2)
        return away, part, ((z - away, z - away >= 0), (z + away, jnp.logical_and(z + away < col_count, away > 0)))

    def line_step(step, start):
        away, part, sides = origins(step)
        for side, (at, valid) in enumerate(sides):
            @pl.when(valid)
            def _():
                if start:
                    @pl.when(away > 0)
                    def _():
                        arrive(at, l, part)

                if side == 0:
                    @pl.when(z + 1 < col_count)
                    def _():
                        send(UP, at, l, part, start)

                @pl.when(jnp.logical_and(z > 0, (away == 0) if side == 0 else True))
                def _():
                    send(DOWN, at, l, part, start)

                @pl.when(jnp.logical_not(jnp.logical_and(at == paired, part == 1)))
                def _():
                    send(CROSS, at, l, part, start)

                send(SIBLING, at, l, part, start)

    def cross_step(step, start):
        away, part, sides = origins(step)
        for at, valid in sides:
            @pl.when(jnp.logical_and(valid, jnp.logical_not(jnp.logical_and(at == paired, part == 1))))
            def _():
                if start:
                    arrive(at, cross, part)
                send(SIBLING, at, cross, part, start)

    def compute(at, part):
        arrive(at, sibling, part)
        arrive(at, cross_sibling, part)

        @pl.when(part == 0)
        def _():
            table = pltpu.make_async_copy(ymeta.at[at], ytable.at[at], local_sem.at[0])
            table.start()
            table.wait()

        def one_row(j, carry):
            i = part * half + j
            wanted = [out_cols_ref[2 * i], out_cols_ref[2 * i + 1]]
            left, right = [], []
            for tile in range(4):
                left.append(yall[at, tile, i])
                first = TILE_COLS * (at * 4 + tile)
                inner = ytable[at, tile, 0, i]
                found = ptable[first // rows, 0, ytable[at, tile, 1, i]]
                right.append(jnp.concatenate(
                    [mall[jnp.where(found == want, inner, row_count * rows)] for want in wanted], axis=1
                ))
            acc[i] += jnp.dot(
                jnp.concatenate(left, axis=1), jnp.concatenate(right, axis=0),
                preferred_element_type=jnp.float32,
            )
            return carry

        lax.fori_loop(0, half, one_row, 0)

    def compute_step(step):
        away, part, sides = origins(step)
        for at, valid in sides:
            @pl.when(jnp.logical_and(valid, jnp.logical_not(jnp.logical_and(at == paired, part == 1))))
            def _():
                compute(at, part)

    def row_copies(other):
        device = (other, z, l)
        blocks = pltpu.make_async_remote_copy(
            src_ref=mall.at[pl.ds(r * rows, rows)],
            dst_ref=mall.at[pl.ds(r * rows, rows)],
            send_sem=row_send.at[other],
            recv_sem=row_recv.at[r],
            device_id=device,
            device_id_type=MESH,
        )
        meta = pltpu.make_async_remote_copy(
            src_ref=pmeta.at[r],
            dst_ref=pmeta.at[r],
            send_sem=rmeta_send.at[other],
            recv_sem=rmeta_recv.at[r],
            device_id=device,
            device_id_type=MESH,
        )
        return blocks, meta

    def row_arrivals(other):
        device = (other, z, l)
        blocks = pltpu.make_async_remote_copy(
            src_ref=mall.at[pl.ds(other * rows, rows)],
            dst_ref=mall.at[pl.ds(other * rows, rows)],
            send_sem=row_send.at[other],
            recv_sem=row_recv.at[other],
            device_id=device,
            device_id_type=MESH,
        )
        meta = pltpu.make_async_remote_copy(
            src_ref=pmeta.at[other],
            dst_ref=pmeta.at[other],
            send_sem=rmeta_send.at[other],
            recv_sem=rmeta_recv.at[other],
            device_id=device,
            device_id_type=MESH,
        )
        return blocks, meta

    def extra(start):
        send(UP, z, cross, 1, start, (r, paired, l))

    last = 2 * col_count

    def advance(step, carry):
        @pl.when(step < last)
        def _():
            line_step(step, True)

        @pl.when(step == 0)
        def _():
            for other in range(1, row_count):
                for copy in row_copies(lax.rem(r + other, row_count)):
                    copy.start()
            mall[row_count * rows] = jnp.zeros(mall.shape[1:], mall.dtype)

            def begin(i, carry):
                own = yall[z, l, i].astype(jnp.float32)
                mine = ycols_ref[i]
                for w in range(2):
                    scale = jnp.where(out_cols_ref[2 * i + w] == mine, -3.0, 0.0)
                    acc[i, :, w * LANES:(w + 1) * LANES] = own * scale
                return carry

            lax.fori_loop(0, rows, begin, 0)

        @pl.when(step == last - 1)
        def _():
            extra(True)

        @pl.when(jnp.logical_and(step >= 2, step < last + 2))
        def _():
            cross_step(step - 2, True)

        @pl.when(step == 3)
        def _():
            for other in range(1, row_count):
                for copy in row_arrivals(lax.rem(r + other, row_count)):
                    copy.wait_recv()
            table = pltpu.make_async_copy(pmeta, ptable, local_sem.at[1])
            table.start()
            table.wait()

        @pl.when(step >= 3)
        def _():
            compute_step(step - 3)

        return carry

    lax.fori_loop(0, last + 3, advance, 0)

    arrive(paired, cross, 1)
    send(SIBLING, paired, cross, 1, True)
    compute(paired, 1)

    def finish(i, carry):
        for w in range(2):
            out_ref[i, w] = (-0.5 * acc[i, :, w * LANES:(w + 1) * LANES]).astype(out_ref.dtype)
        return carry

    lax.fori_loop(0, rows, finish, 0)

    def drain(step, carry):
        line_step(step, False)
        cross_step(step, False)
        return carry

    lax.fori_loop(0, last, drain, 0)
    extra(False)
    send(SIBLING, paired, cross, 1, False)
    for other in range(1, row_count):
        for copy in row_copies(lax.rem(r + other, row_count)):
            copy.wait_send()


def shards(row_count, col_count, y_blocks, y_cols, prod_blocks, prod_cols, out_cols):
    rows, _, size, _ = y_blocks.shape

    def lane_rows(cols):
        table = jnp.concatenate([cols.reshape(1, rows), cols.reshape(1, rows) % rows], axis=0)
        return jnp.pad(table, ((0, 6), (0, LANES - rows)))

    anywhere = pl.BlockSpec(memory_space=pl.ANY)
    scalars = pl.BlockSpec(memory_space=pltpu.SMEM)
    dma = pltpu.SemaphoreType.DMA
    y_next = pl.pallas_call(
        functools.partial(kernel, row_count, col_count),
        out_shape=jax.ShapeDtypeStruct((rows, 2, size, size), jnp.bfloat16),
        in_specs=[anywhere] * 4 + [scalars] * 2,
        out_specs=pl.BlockSpec(memory_space=pltpu.VMEM),
        scratch_shapes=[
            pltpu.VMEM((col_count, 4, rows, size, size), jnp.bfloat16),
            pltpu.VMEM((row_count * rows + 1, size, size), jnp.bfloat16),
            pltpu.VMEM((rows, size, 2 * size), jnp.float32),
            pltpu.VMEM((col_count, 4, 8, LANES), jnp.int32),
            pltpu.VMEM((row_count, 8, LANES), jnp.int32),
            pltpu.SMEM((col_count, 4, 8, LANES), jnp.int32),
            pltpu.SMEM((row_count, 8, LANES), jnp.int32),
            dma((4, col_count, 4, 2)),
            dma((col_count, 4, 2)),
            dma((4, col_count, 4)),
            dma((col_count, 4)),
            dma((row_count,)),
            dma((row_count,)),
            dma((row_count,)),
            dma((row_count,)),
            dma((4,)),
        ],
        compiler_params=pltpu.CompilerParams(
            collective_id=0, has_side_effects=True, vmem_limit_bytes=56 * 1024 * 1024
        ),
    )(
        y_blocks.reshape(rows, size, size), prod_blocks.reshape(rows, size, size),
        lane_rows(y_cols), lane_rows(prod_cols), y_cols.reshape(rows), out_cols.reshape(2 * rows),
    )
    return y_next.reshape(rows, 1, 2, size, size)


def solution(mesh):
    placed = (
        P("rows", ("cols", "layers"), None, None),
        P("rows", ("cols", "layers")),
        P("rows", ("cols", "layers"), None, None),
        P("rows", ("cols", "layers")),
        P("rows", ("cols", "layers"), None),
    )
    return jax.shard_map(
        functools.partial(shards, mesh.shape["rows"], mesh.shape["cols"]),
        mesh=mesh,
        in_specs=placed,
        out_specs=P("rows", ("cols", "layers"), None, None, None),
        check_vma=False,
    )
```

```python
import functools

import jax
import jax.numpy as jnp
from jax import lax
from jax.experimental import pallas as pl
from jax.experimental.pallas import tpu as pltpu
from jax.sharding import PartitionSpec as P

TILE_COLS = 6
LANES = 128
PARTS = 4
TOGETHER = 3
MESH = pl.DeviceIdType.MESH
UP, DOWN, CROSS, SIBLING = range(4)


def kernel(
    row_count, col_count, y_ref, m_ref, table_ref, out_ref,
    yall, mall, acc, ytables, rtables, ytable, rtable,
    send_sem, recv_sem, tsend_sem, trecv_sem, row_send, row_recv, rtable_send, rtable_recv, local_sem,
):
    rows = y_ref.shape[0]
    piece = rows // PARTS
    r, z, l = lax.axis_index("rows"), lax.axis_index("cols"), lax.axis_index("layers")
    cross = lax.rem(l + 2, 4)
    sibling = l + 1 - 2 * lax.rem(l, 2)
    cross_sibling = lax.rem(sibling + 2, 4)
    paired = z + 1 - 2 * lax.rem(z, 2)
    targets = {UP: (r, z + 1, l), DOWN: (r, z - 1, l), CROSS: (r, z, cross), SIBLING: (r, z, sibling)}

    own_copies = [
        pltpu.make_async_copy(y_ref, yall.at[z, l], local_sem.at[0]),
        pltpu.make_async_copy(m_ref, mall.at[pl.ds(r * rows, rows)], local_sem.at[1]),
        pltpu.make_async_copy(table_ref, ytables.at[z, l], local_sem.at[2]),
        pltpu.make_async_copy(table_ref, rtables.at[r], local_sem.at[3]),
        pltpu.make_async_copy(table_ref, rtable.at[row_count], local_sem.at[4]),
    ]
    for copy in own_copies:
        copy.start()

    barrier = pltpu.get_barrier_semaphore()

    def greet(device):
        pl.semaphore_signal(barrier, inc=1, device_id=device, device_id_type=MESH)

    greet(targets[CROSS])
    greet(targets[SIBLING])
    for step in range(1, row_count):
        greet((lax.rem(r + step, row_count), z, l))

    @pl.when(z + 1 < col_count)
    def _():
        greet(targets[UP])

    @pl.when(z > 0)
    def _():
        greet(targets[DOWN])

    line_peers = jnp.where(z > 0, 1, 0) + jnp.where(z + 1 < col_count, 1, 0)
    pl.semaphore_wait(barrier, 1 + row_count + line_peers)

    for copy in own_copies:
        copy.wait()

    def chunk_copy(way, at, tile, part, device):
        return pltpu.make_async_remote_copy(
            src_ref=yall.at[at, tile, pl.ds(part * piece, piece)],
            dst_ref=yall.at[at, tile, pl.ds(part * piece, piece)],
            send_sem=send_sem.at[way, at, tile, part],
            recv_sem=recv_sem.at[at, tile, part],
            device_id=device,
            device_id_type=MESH,
        )

    def table_copy(way, at, tile, device):
        return pltpu.make_async_remote_copy(
            src_ref=ytables.at[at, tile],
            dst_ref=ytables.at[at, tile],
            send_sem=tsend_sem.at[way, at, tile],
            recv_sem=trecv_sem.at[at, tile],
            device_id=device,
            device_id_type=MESH,
        )

    def send(way, at, tile, part, start, device=None):
        device = targets[way] if device is None else device
        chunk = chunk_copy(way, at, tile, part, device)
        if start:
            chunk.start()
        else:
            chunk.wait_send()

        @pl.when(part == 0)
        def _():
            table = table_copy(way, at, tile, device)
            if start:
                table.start()
            else:
                table.wait_send()

    def arrive(at, tile, part):
        chunk_copy(SIBLING, at, tile, part, targets[SIBLING]).wait_recv()

        @pl.when(part == 0)
        def _():
            table_copy(SIBLING, at, tile, targets[SIBLING]).wait_recv()

    def origins(step):
        away, part = step // PARTS, lax.rem(step, PARTS)
        return away, part, ((z - away, z - away >= 0), (z + away, jnp.logical_and(z + away < col_count, away > 0)))

    def by_cross_link(at, part):
        return jnp.logical_not(jnp.logical_and(at == paired, part >= PARTS // 2))

    def line_step(step, start):
        away, part, sides = origins(step)
        for side, (at, valid) in enumerate(sides):
            @pl.when(valid)
            def _():
                if start:
                    @pl.when(away > 0)
                    def _():
                        arrive(at, l, part)

                if side == 0:
                    @pl.when(z + 1 < col_count)
                    def _():
                        send(UP, at, l, part, start)

                @pl.when(jnp.logical_and(z > 0, (away == 0) if side == 0 else True))
                def _():
                    send(DOWN, at, l, part, start)

                @pl.when(by_cross_link(at, part))
                def _():
                    send(CROSS, at, l, part, start)

                send(SIBLING, at, l, part, start)

    def cross_step(step, start):
        away, part, sides = origins(step)
        for at, valid in sides:
            @pl.when(jnp.logical_and(valid, by_cross_link(at, part)))
            def _():
                if start:
                    arrive(at, cross, part)
                send(SIBLING, at, cross, part, start)

    def compute(at, part, mine, other):
        arrive(at, other, part)

        @pl.when(part == 0)
        def _():
            copies = [
                pltpu.make_async_copy(ytables.at[at, tile], ytable.at[at, tile], local_sem.at[n])
                for n, tile in enumerate((mine, other))
            ]
            for copy in copies:
                copy.start()
            for copy in copies:
                copy.wait()

        def some_rows(j, carry):
            sums = []
            for u in range(TOGETHER):
                i = part * piece + j * TOGETHER + u
                wanted = [rtable[row_count, 3, i], rtable[row_count, 4, i]]
                left, right = [], []
                for tile in (mine, other):
                    left.append(yall[at, tile, i])
                    first = TILE_COLS * (at * 4 + tile)
                    inner = ytable[at, tile, 0, i]
                    found = rtable[first // rows, 2, ytable[at, tile, 1, i]]
                    right.append(jnp.concatenate(
                        [mall[jnp.where(found == want, inner, row_count * rows)] for want in wanted], axis=1
                    ))
                sums.append(acc[i] + jnp.dot(
                    jnp.concatenate(left, axis=1), jnp.concatenate(right, axis=0),
                    preferred_element_type=jnp.float32,
                ))
            for u in range(TOGETHER):
                acc[part * piece + j * TOGETHER + u] = sums[u]
            return carry

        lax.fori_loop(0, piece // TOGETHER, some_rows, 0)

    def compute_line(step, carry):
        away, part, sides = origins(step)
        for at, valid in sides:
            @pl.when(valid)
            def _():
                compute(at, part, l, sibling)
        return carry

    def compute_cross(step, carry):
        away, part, sides = origins(step)
        for at, valid in sides:
            @pl.when(jnp.logical_and(valid, by_cross_link(at, part)))
            def _():
                compute(at, part, cross, cross_sibling)
        return carry

    def row_copies(owner, other):
        device = (other, z, l)
        owned = pl.ds(owner * rows, rows)
        key = jnp.where(owner == r, other, owner)
        blocks = pltpu.make_async_remote_copy(
            src_ref=mall.at[owned],
            dst_ref=mall.at[owned],
            send_sem=row_send.at[key],
            recv_sem=row_recv.at[owner],
            device_id=device,
            device_id_type=MESH,
        )
        table = pltpu.make_async_remote_copy(
            src_ref=rtables.at[owner],
            dst_ref=rtables.at[owner],
            send_sem=rtable_send.at[key],
            recv_sem=rtable_recv.at[owner],
            device_id=device,
            device_id_type=MESH,
        )
        return blocks, table

    def extra(part, start):
        send(UP, z, cross, part, start, (r, paired, l))

    last = PARTS * col_count
    first_sums = last // 2
    lag = PARTS + 1

    def advance(step, carry):
        @pl.when(step < last)
        def _():
            line_step(step, True)

        @pl.when(step == 0)
        def _():
            for other in range(1, row_count):
                for copy in row_copies(r, lax.rem(r + other, row_count)):
                    copy.start()
            mall[row_count * rows] = jnp.zeros(mall.shape[1:], mall.dtype)

            def begin(i, carry):
                own = yall[z, l, i].astype(jnp.float32)
                for w in range(2):
                    scale = jnp.where(rtable[row_count, 3 + w, i] == rtable[row_count, 0, i], -3.0, 0.0)
                    acc[i, :, w * LANES:(w + 1) * LANES] = own * scale
                return carry

            lax.fori_loop(0, rows, begin, 0)

        @pl.when(step == last - 1)
        def _():
            for part in range(PARTS // 2, PARTS):
                extra(part, True)

        @pl.when(jnp.logical_and(step >= lag, step < last + lag))
        def _():
            cross_step(step - lag, True)

        @pl.when(step == first_sums)
        def _():
            for n in range(1, row_count):
                other = lax.rem(r + n, row_count)
                for copy in row_copies(other, other):
                    copy.wait_recv()
            copies = [pltpu.make_async_copy(rtables.at[n], rtable.at[n], local_sem.at[n]) for n in range(row_count)]
            for copy in copies:
                copy.start()
            for copy in copies:
                copy.wait()

        def reached(behind, now):
            return jnp.clip(jnp.minimum(now - behind, 2 * (now - first_sums + 1)), 0, last)

        lax.fori_loop(reached(0, step - 1), reached(0, step), compute_line, 0)
        lax.fori_loop(reached(lag, step - 1), reached(lag, step), compute_cross, 0)
        return carry

    lax.fori_loop(0, last + lag + 1, advance, 0)

    for part in range(PARTS // 2, PARTS):
        arrive(paired, cross, part)
        send(SIBLING, paired, cross, part, True)

    def compute_extra(part, carry):
        compute(paired, part, cross, cross_sibling)
        return carry

    lax.fori_loop(PARTS // 2, PARTS, compute_extra, 0)

    def finish(i, carry):
        for w in range(2):
            out_ref[i, w] = (-0.5 * acc[i, :, w * LANES:(w + 1) * LANES]).astype(out_ref.dtype)
        return carry

    lax.fori_loop(0, rows, finish, 0)

    def drain(step, carry):
        line_step(step, False)
        cross_step(step, False)
        return carry

    lax.fori_loop(0, last, drain, 0)
    for part in range(PARTS // 2, PARTS):
        extra(part, False)
        send(SIBLING, paired, cross, part, False)
    for n in range(1, row_count):
        for copy in row_copies(r, lax.rem(r + n, row_count)):
            copy.wait_send()


def shards(row_count, col_count, y_blocks, y_cols, prod_blocks, prod_cols, out_cols):
    rows, _, size, _ = y_blocks.shape
    table = jnp.concatenate([y_cols, y_cols % rows, prod_cols, out_cols[:, 0]], axis=1)
    table = jnp.pad(table, ((0, LANES - rows), (0, 3))).T
    anywhere = pl.BlockSpec(memory_space=pl.ANY)
    dma = pltpu.SemaphoreType.DMA
    y_next = pl.pallas_call(
        functools.partial(kernel, row_count, col_count),
        out_shape=jax.ShapeDtypeStruct((rows, 2, size, size), jnp.bfloat16),
        in_specs=[anywhere] * 3,
        out_specs=pl.BlockSpec(memory_space=pltpu.VMEM),
        scratch_shapes=[
            pltpu.VMEM((col_count, 4, rows, size, size), jnp.bfloat16),
            pltpu.VMEM((row_count * rows + 1, size, size), jnp.bfloat16),
            pltpu.VMEM((rows, size, 2 * size), jnp.float32),
            pltpu.VMEM((col_count, 4, 8, LANES), jnp.int32),
            pltpu.VMEM((row_count, 8, LANES), jnp.int32),
            pltpu.SMEM((col_count, 4, 8, LANES), jnp.int32),
            pltpu.SMEM((row_count + 1, 8, LANES), jnp.int32),
            dma((4, col_count, 4, PARTS)),
            dma((col_count, 4, PARTS)),
            dma((4, col_count, 4)),
            dma((col_count, 4)),
            dma((row_count,)),
            dma((row_count,)),
            dma((row_count,)),
            dma((row_count,)),
            dma((max(5, row_count),)),
        ],
        compiler_params=pltpu.CompilerParams(
            collective_id=0, has_side_effects=True, vmem_limit_bytes=56 * 1024 * 1024
        ),
    )(y_blocks.reshape(rows, size, size), prod_blocks.reshape(rows, size, size), table)
    return y_next.reshape(rows, 1, 2, size, size)


def solution(mesh):
    placed = (
        P("rows", ("cols", "layers"), None, None),
        P("rows", ("cols", "layers")),
        P("rows", ("cols", "layers"), None, None),
        P("rows", ("cols", "layers")),
        P("rows", ("cols", "layers"), None),
    )
    return jax.shard_map(
        functools.partial(shards, mesh.shape["rows"], mesh.shape["cols"]),
        mesh=mesh,
        in_specs=placed,
        out_specs=P("rows", ("cols", "layers"), None, None, None),
        check_vma=False,
    )
```

```python
import functools

import jax
import jax.numpy as jnp
from jax import lax
from jax.experimental import pallas as pl
from jax.experimental.pallas import tpu as pltpu
from jax.sharding import PartitionSpec as P

TILE_COLS = 6
LANES = 128
PARTS = 8
TOGETHER = 3
MESH = pl.DeviceIdType.MESH
UP, DOWN, CROSS, SIBLING = range(4)


def kernel(
    row_count, col_count, y_ref, m_ref, table_ref, out_ref,
    yall, mall, acc, outs, ytables, rtables, ytable, rtable,
    send_sem, recv_sem, tsend_sem, trecv_sem, row_send, row_recv, rtable_send, rtable_recv, local_sem, out_sem,
):
    rows = y_ref.shape[0]
    piece = rows // PARTS
    r, z, l = lax.axis_index("rows"), lax.axis_index("cols"), lax.axis_index("layers")
    cross = lax.rem(l + 2, 4)
    sibling = l + 1 - 2 * lax.rem(l, 2)
    cross_sibling = lax.rem(sibling + 2, 4)
    paired = z + 1 - 2 * lax.rem(z, 2)
    targets = {UP: (r, z + 1, l), DOWN: (r, z - 1, l), CROSS: (r, z, cross), SIBLING: (r, z, sibling)}

    own_copies = [
        pltpu.make_async_copy(y_ref, yall.at[z, l], local_sem.at[0]),
        pltpu.make_async_copy(m_ref, mall.at[pl.ds(r * rows, rows)], local_sem.at[1]),
        pltpu.make_async_copy(table_ref, ytables.at[z, l], local_sem.at[2]),
        pltpu.make_async_copy(table_ref, rtables.at[r], local_sem.at[3]),
        pltpu.make_async_copy(table_ref, rtable.at[row_count], local_sem.at[4]),
    ]
    for copy in own_copies:
        copy.start()

    barrier = pltpu.get_barrier_semaphore()

    def greet(device):
        pl.semaphore_signal(barrier, inc=1, device_id=device, device_id_type=MESH)

    greet(targets[CROSS])
    greet(targets[SIBLING])
    for step in range(1, row_count):
        greet((lax.rem(r + step, row_count), z, l))

    @pl.when(z + 1 < col_count)
    def _():
        greet(targets[UP])

    @pl.when(z > 0)
    def _():
        greet(targets[DOWN])

    line_peers = jnp.where(z > 0, 1, 0) + jnp.where(z + 1 < col_count, 1, 0)
    pl.semaphore_wait(barrier, 1 + row_count + line_peers)

    for copy in own_copies:
        copy.wait()

    def chunk_copy(way, at, tile, part, device):
        return pltpu.make_async_remote_copy(
            src_ref=yall.at[at, tile, pl.ds(part * piece, piece)],
            dst_ref=yall.at[at, tile, pl.ds(part * piece, piece)],
            send_sem=send_sem.at[way, at, tile, part],
            recv_sem=recv_sem.at[at, tile, part],
            device_id=device,
            device_id_type=MESH,
        )

    def table_copy(way, at, tile, device):
        return pltpu.make_async_remote_copy(
            src_ref=ytables.at[at, tile],
            dst_ref=ytables.at[at, tile],
            send_sem=tsend_sem.at[way, at, tile],
            recv_sem=trecv_sem.at[at, tile],
            device_id=device,
            device_id_type=MESH,
        )

    def send(way, at, tile, part, start, device=None):
        device = targets[way] if device is None else device
        chunk = chunk_copy(way, at, tile, part, device)
        if start:
            chunk.start()
        else:
            chunk.wait_send()

        @pl.when(part == 0)
        def _():
            table = table_copy(way, at, tile, device)
            if start:
                table.start()
            else:
                table.wait_send()

    def arrive(at, tile, part):
        chunk_copy(SIBLING, at, tile, part, targets[SIBLING]).wait_recv()

        @pl.when(part == 0)
        def _():
            table_copy(SIBLING, at, tile, targets[SIBLING]).wait_recv()

    def origins(step):
        away, part = step // PARTS, lax.rem(step, PARTS)
        return away, part, ((z - away, z - away >= 0), (z + away, jnp.logical_and(z + away < col_count, away > 0)))

    def by_cross_link(at, part):
        return jnp.logical_not(jnp.logical_and(at == paired, part >= PARTS // 2))

    def line_step(step, start):
        away, part, sides = origins(step)
        for side, (at, valid) in enumerate(sides):
            @pl.when(valid)
            def _():
                if start:
                    @pl.when(away > 0)
                    def _():
                        arrive(at, l, part)

                if side == 0:
                    @pl.when(z + 1 < col_count)
                    def _():
                        send(UP, at, l, part, start)

                @pl.when(jnp.logical_and(z > 0, (away == 0) if side == 0 else True))
                def _():
                    send(DOWN, at, l, part, start)

                @pl.when(by_cross_link(at, part))
                def _():
                    send(CROSS, at, l, part, start)

                send(SIBLING, at, l, part, start)

    def cross_step(step, start):
        away, part, sides = origins(step)
        for at, valid in sides:
            @pl.when(jnp.logical_and(valid, by_cross_link(at, part)))
            def _():
                if start:
                    arrive(at, cross, part)
                send(SIBLING, at, cross, part, start)

    def compute(at, part, mine, other):
        arrive(at, other, part)

        @pl.when(part == 0)
        def _():
            copies = [
                pltpu.make_async_copy(ytables.at[at, tile], ytable.at[at, tile], local_sem.at[n])
                for n, tile in enumerate((mine, other))
            ]
            for copy in copies:
                copy.start()
            for copy in copies:
                copy.wait()

        def some_rows(j, carry):
            sums = []
            for u in range(TOGETHER):
                i = part * piece + j * TOGETHER + u
                wanted = [rtable[row_count, 3, i], rtable[row_count, 4, i]]
                left, right = [], []
                for tile in (mine, other):
                    left.append(yall[at, tile, i])
                    first = TILE_COLS * (at * 4 + tile)
                    inner = ytable[at, tile, 0, i]
                    found = rtable[first // rows, 2, ytable[at, tile, 1, i]]
                    right.append(jnp.concatenate(
                        [mall[jnp.where(found == want, inner, row_count * rows)] for want in wanted], axis=1
                    ))
                sums.append(acc[i] + jnp.dot(
                    jnp.concatenate(left, axis=1), jnp.concatenate(right, axis=0),
                    preferred_element_type=jnp.float32,
                ))
            for u in range(TOGETHER):
                acc[part * piece + j * TOGETHER + u] = sums[u]
            return carry

        lax.fori_loop(0, piece // TOGETHER, some_rows, 0)

    def compute_line(step, carry):
        away, part, sides = origins(step)
        for at, valid in sides:
            @pl.when(valid)
            def _():
                compute(at, part, l, sibling)
        return carry

    def compute_cross(step, carry):
        away, part, sides = origins(step)
        for at, valid in sides:
            @pl.when(jnp.logical_and(valid, by_cross_link(at, part)))
            def _():
                compute(at, part, cross, cross_sibling)
        return carry

    def row_copies(owner, other):
        device = (other, z, l)
        owned = pl.ds(owner * rows, rows)
        key = jnp.where(owner == r, other, owner)
        blocks = pltpu.make_async_remote_copy(
            src_ref=mall.at[owned],
            dst_ref=mall.at[owned],
            send_sem=row_send.at[key],
            recv_sem=row_recv.at[owner],
            device_id=device,
            device_id_type=MESH,
        )
        table = pltpu.make_async_remote_copy(
            src_ref=rtables.at[owner],
            dst_ref=rtables.at[owner],
            send_sem=rtable_send.at[key],
            recv_sem=rtable_recv.at[owner],
            device_id=device,
            device_id_type=MESH,
        )
        return blocks, table

    def extra(part, start):
        send(UP, z, cross, part, start, (r, paired, l))

    last = PARTS * col_count
    first_sums = last // 2
    lag = PARTS + 1

    def advance(step, carry):
        @pl.when(step < last)
        def _():
            line_step(step, True)

        @pl.when(step == 0)
        def _():
            for other in range(1, row_count):
                for copy in row_copies(r, lax.rem(r + other, row_count)):
                    copy.start()
            mall[row_count * rows] = jnp.zeros(mall.shape[1:], mall.dtype)

            def begin(i, carry):
                own = yall[z, l, i].astype(jnp.float32)
                for w in range(2):
                    scale = jnp.where(rtable[row_count, 3 + w, i] == rtable[row_count, 0, i], -3.0, 0.0)
                    acc[i, :, w * LANES:(w + 1) * LANES] = own * scale
                return carry

            lax.fori_loop(0, rows, begin, 0)

        @pl.when(step == PARTS * (jnp.maximum(z, col_count - 1 - z) + 1) - 1)
        def _():
            for part in range(PARTS // 2, PARTS):
                extra(part, True)

        @pl.when(jnp.logical_and(step >= lag, step < last + lag))
        def _():
            cross_step(step - lag, True)

        @pl.when(step == first_sums)
        def _():
            for n in range(1, row_count):
                other = lax.rem(r + n, row_count)
                for copy in row_copies(other, other):
                    copy.wait_recv()
            copies = [pltpu.make_async_copy(rtables.at[n], rtable.at[n], local_sem.at[n]) for n in range(row_count)]
            for copy in copies:
                copy.start()
            for copy in copies:
                copy.wait()

        def reached(behind, now):
            return jnp.clip(jnp.minimum(now - behind, 2 * (now - first_sums + 1)), 0, last)

        lax.fori_loop(reached(0, step - 1), reached(0, step), compute_line, 0)
        lax.fori_loop(reached(lag, step - 1), reached(lag, step), compute_cross, 0)
        return carry

    lax.fori_loop(0, last + lag + 1, advance, 0)

    def out_copy(part):
        some = pl.ds(part * piece, piece)
        return pltpu.make_async_copy(outs.at[some], out_ref.at[some], out_sem.at[part])

    def finish(part, carry):
        def one_row(j, carry):
            i = part * piece + j
            for w in range(2):
                outs[i, w] = (-0.5 * acc[i, :, w * LANES:(w + 1) * LANES]).astype(outs.dtype)
            return carry

        lax.fori_loop(0, piece, one_row, 0)
        out_copy(part).start()
        return carry

    lax.fori_loop(0, PARTS // 2, finish, 0)

    def close(part, carry):
        @pl.when(part < PARTS)
        def _():
            arrive(paired, cross, part)
            send(SIBLING, paired, cross, part, True)

        @pl.when(part > PARTS // 2)
        def _():
            compute(paired, part - 1, cross, cross_sibling)
            finish(part - 1, 0)

        return carry

    lax.fori_loop(PARTS // 2, PARTS + 1, close, 0)

    def drain(step, carry):
        line_step(step, False)
        cross_step(step, False)
        return carry

    lax.fori_loop(0, last, drain, 0)
    for part in range(PARTS // 2, PARTS):
        extra(part, False)
        send(SIBLING, paired, cross, part, False)
    for n in range(1, row_count):
        for copy in row_copies(r, lax.rem(r + n, row_count)):
            copy.wait_send()
    for part in range(PARTS):
        out_copy(part).wait()


def shards(row_count, col_count, y_blocks, y_cols, prod_blocks, prod_cols, out_cols):
    rows, _, size, _ = y_blocks.shape
    table = jnp.concatenate([y_cols, y_cols % rows, prod_cols, out_cols[:, 0]], axis=1)
    table = jnp.pad(table, ((0, LANES - rows), (0, 3))).T
    anywhere = pl.BlockSpec(memory_space=pl.ANY)
    dma = pltpu.SemaphoreType.DMA
    y_next = pl.pallas_call(
        functools.partial(kernel, row_count, col_count),
        out_shape=jax.ShapeDtypeStruct((rows, 2, size, size), jnp.bfloat16),
        in_specs=[anywhere] * 3,
        out_specs=anywhere,
        scratch_shapes=[
            pltpu.VMEM((col_count, 4, rows, size, size), jnp.bfloat16),
            pltpu.VMEM((row_count * rows + 1, size, size), jnp.bfloat16),
            pltpu.VMEM((rows, size, 2 * size), jnp.float32),
            pltpu.VMEM((rows, 2, size, size), jnp.bfloat16),
            pltpu.VMEM((col_count, 4, 8, LANES), jnp.int32),
            pltpu.VMEM((row_count, 8, LANES), jnp.int32),
            pltpu.SMEM((col_count, 4, 8, LANES), jnp.int32),
            pltpu.SMEM((row_count + 1, 8, LANES), jnp.int32),
            dma((4, col_count, 4, PARTS)),
            dma((col_count, 4, PARTS)),
            dma((4, col_count, 4)),
            dma((col_count, 4)),
            dma((row_count,)),
            dma((row_count,)),
            dma((row_count,)),
            dma((row_count,)),
            dma((max(5, row_count),)),
            dma((PARTS,)),
        ],
        compiler_params=pltpu.CompilerParams(
            collective_id=0, has_side_effects=True, vmem_limit_bytes=56 * 1024 * 1024
        ),
    )(y_blocks.reshape(rows, size, size), prod_blocks.reshape(rows, size, size), table)
    return y_next.reshape(rows, 1, 2, size, size)


def solution(mesh):
    placed = (
        P("rows", ("cols", "layers"), None, None),
        P("rows", ("cols", "layers")),
        P("rows", ("cols", "layers"), None, None),
        P("rows", ("cols", "layers")),
        P("rows", ("cols", "layers"), None),
    )
    return jax.shard_map(
        functools.partial(shards, mesh.shape["rows"], mesh.shape["cols"]),
        mesh=mesh,
        in_specs=placed,
        out_specs=P("rows", ("cols", "layers"), None, None, None),
        check_vma=False,
    )
```

```python
import functools

import jax
import jax.numpy as jnp
from jax import lax
from jax.experimental import pallas as pl
from jax.experimental.pallas import tpu as pltpu
from jax.sharding import PartitionSpec as P

TILE_COLS = 6
LANES = 128
PARTS = 8
WINDOW = 2
TOGETHER = 3
MESH = pl.DeviceIdType.MESH
UP, DOWN, CROSS, SIBLING = range(4)


def kernel(
    row_count, col_count, y_ref, m_ref, table_ref, out_ref,
    yall, mall, acc, outs, ytables, rtables, ytable, rtable,
    send_sem, recv_sem, tsend_sem, trecv_sem, row_send, row_recv, rtable_send, rtable_recv, local_sem, out_sem,
):
    rows = y_ref.shape[0]
    piece = rows // PARTS
    r, z, l = lax.axis_index("rows"), lax.axis_index("cols"), lax.axis_index("layers")
    cross = lax.rem(l + 2, 4)
    sibling = l + 1 - 2 * lax.rem(l, 2)
    cross_sibling = lax.rem(sibling + 2, 4)
    paired = z + 1 - 2 * lax.rem(z, 2)
    targets = {UP: (r, z + 1, l), DOWN: (r, z - 1, l), CROSS: (r, z, cross), SIBLING: (r, z, sibling)}

    own_copies = [
        pltpu.make_async_copy(y_ref, yall.at[z, l], local_sem.at[0]),
        pltpu.make_async_copy(m_ref, mall.at[pl.ds(r * rows, rows)], local_sem.at[1]),
        pltpu.make_async_copy(table_ref, ytables.at[z, l], local_sem.at[2]),
        pltpu.make_async_copy(table_ref, rtables.at[r], local_sem.at[3]),
        pltpu.make_async_copy(table_ref, rtable.at[row_count], local_sem.at[4]),
    ]
    for copy in own_copies:
        copy.start()

    barrier = pltpu.get_barrier_semaphore()

    def greet(device):
        pl.semaphore_signal(barrier, inc=1, device_id=device, device_id_type=MESH)

    greet(targets[CROSS])
    greet(targets[SIBLING])
    for step in range(1, row_count):
        greet((lax.rem(r + step, row_count), z, l))

    @pl.when(z + 1 < col_count)
    def _():
        greet(targets[UP])

    @pl.when(z > 0)
    def _():
        greet(targets[DOWN])

    line_peers = jnp.where(z > 0, 1, 0) + jnp.where(z + 1 < col_count, 1, 0)
    pl.semaphore_wait(barrier, 1 + row_count + line_peers)

    for copy in own_copies:
        copy.wait()

    def chunk_copy(way, at, tile, part, device):
        return pltpu.make_async_remote_copy(
            src_ref=yall.at[at, tile, pl.ds(part * piece, piece)],
            dst_ref=yall.at[at, tile, pl.ds(part * piece, piece)],
            send_sem=send_sem.at[way, at, tile, part],
            recv_sem=recv_sem.at[at, tile, part],
            device_id=device,
            device_id_type=MESH,
        )

    def table_copy(way, at, tile, device):
        return pltpu.make_async_remote_copy(
            src_ref=ytables.at[at, tile],
            dst_ref=ytables.at[at, tile],
            send_sem=tsend_sem.at[way, at, tile],
            recv_sem=trecv_sem.at[at, tile],
            device_id=device,
            device_id_type=MESH,
        )

    def send(way, at, tile, part, start, device=None):
        device = targets[way] if device is None else device
        chunk = chunk_copy(way, at, tile, part, device)
        if start:
            chunk.start()
        else:
            chunk.wait_send()

        @pl.when(part == 0)
        def _():
            table = table_copy(way, at, tile, device)
            if start:
                table.start()
            else:
                table.wait_send()

    def arrive(at, tile, part):
        chunk_copy(SIBLING, at, tile, part, targets[SIBLING]).wait_recv()

        @pl.when(part == 0)
        def _():
            table_copy(SIBLING, at, tile, targets[SIBLING]).wait_recv()

    def origins(step):
        away, part = step // PARTS, lax.rem(step, PARTS)
        return away, part, ((z - away, z - away >= 0), (z + away, jnp.logical_and(z + away < col_count, away > 0)))

    def by_cross_link(at, part):
        return jnp.logical_not(jnp.logical_and(at == paired, part >= PARTS // 2))

    def line_step(step, start):
        away, part, sides = origins(step)
        for side, (at, valid) in enumerate(sides):
            @pl.when(valid)
            def _():
                if start:
                    @pl.when(away > 0)
                    def _():
                        arrive(at, l, part)

                if side == 0:
                    @pl.when(z + 1 < col_count)
                    def _():
                        send(UP, at, l, part, start)

                @pl.when(jnp.logical_and(z > 0, (away == 0) if side == 0 else True))
                def _():
                    send(DOWN, at, l, part, start)

                @pl.when(by_cross_link(at, part))
                def _():
                    send(CROSS, at, l, part, start)

                send(SIBLING, at, l, part, start)

    def cross_step(step, start):
        away, part, sides = origins(step)
        for at, valid in sides:
            @pl.when(jnp.logical_and(valid, by_cross_link(at, part)))
            def _():
                if start:
                    arrive(at, cross, part)
                send(SIBLING, at, cross, part, start)

    def compute(at, part, mine, other):
        arrive(at, other, part)

        @pl.when(part == 0)
        def _():
            copies = [
                pltpu.make_async_copy(ytables.at[at, tile], ytable.at[at, tile], local_sem.at[n])
                for n, tile in enumerate((mine, other))
            ]
            for copy in copies:
                copy.start()
            for copy in copies:
                copy.wait()

        def some_rows(j, carry):
            sums = []
            for u in range(TOGETHER):
                i = part * piece + j * TOGETHER + u
                wanted = [rtable[row_count, 3, i], rtable[row_count, 4, i]]
                left, right = [], []
                for tile in (mine, other):
                    left.append(yall[at, tile, i])
                    first = TILE_COLS * (at * 4 + tile)
                    inner = ytable[at, tile, 0, i]
                    found = rtable[first // rows, 2, ytable[at, tile, 1, i]]
                    right.append(jnp.concatenate(
                        [mall[jnp.where(found == want, inner, row_count * rows)] for want in wanted], axis=1
                    ))
                sums.append(acc[i] + jnp.dot(
                    jnp.concatenate(left, axis=1), jnp.concatenate(right, axis=0),
                    preferred_element_type=jnp.float32,
                ))
            for u in range(TOGETHER):
                acc[part * piece + j * TOGETHER + u] = sums[u]
            return carry

        lax.fori_loop(0, piece // TOGETHER, some_rows, 0)

    def compute_line(step, carry):
        away, part, sides = origins(step)
        for at, valid in sides:
            @pl.when(valid)
            def _():
                compute(at, part, l, sibling)
        return carry

    def compute_cross(step, carry):
        away, part, sides = origins(step)
        for at, valid in sides:
            @pl.when(jnp.logical_and(valid, by_cross_link(at, part)))
            def _():
                compute(at, part, cross, cross_sibling)
        return carry

    def row_copies(owner, other):
        device = (other, z, l)
        owned = pl.ds(owner * rows, rows)
        key = jnp.where(owner == r, other, owner)
        blocks = pltpu.make_async_remote_copy(
            src_ref=mall.at[owned],
            dst_ref=mall.at[owned],
            send_sem=row_send.at[key],
            recv_sem=row_recv.at[owner],
            device_id=device,
            device_id_type=MESH,
        )
        table = pltpu.make_async_remote_copy(
            src_ref=rtables.at[owner],
            dst_ref=rtables.at[owner],
            send_sem=rtable_send.at[key],
            recv_sem=rtable_recv.at[owner],
            device_id=device,
            device_id_type=MESH,
        )
        return blocks, table

    def extra(part, start):
        send(UP, z, cross, part, start, (r, paired, l))

    last = PARTS * col_count
    first_sums = last // 2
    lag = PARTS + 1

    def advance(step, carry):
        @pl.when(jnp.logical_and(step >= WINDOW, step < PARTS))
        def _():
            line_step(step - WINDOW, False)

        @pl.when(step < last)
        def _():
            line_step(step, True)

        @pl.when(step == 0)
        def _():
            for other in range(1, row_count):
                for copy in row_copies(r, lax.rem(r + other, row_count)):
                    copy.start()
            mall[row_count * rows] = jnp.zeros(mall.shape[1:], mall.dtype)

            def begin(i, carry):
                own = yall[z, l, i].astype(jnp.float32)
                for w in range(2):
                    scale = jnp.where(rtable[row_count, 3 + w, i] == rtable[row_count, 0, i], -3.0, 0.0)
                    acc[i, :, w * LANES:(w + 1) * LANES] = own * scale
                return carry

            lax.fori_loop(0, rows, begin, 0)

        @pl.when(step == last - 5)
        def _():
            for part in range(PARTS // 2, PARTS):
                extra(part, True)

        @pl.when(jnp.logical_and(step >= lag, step < last + lag))
        def _():
            cross_step(step - lag, True)

        @pl.when(step == first_sums)
        def _():
            for n in range(1, row_count):
                other = lax.rem(r + n, row_count)
                for copy in row_copies(other, other):
                    copy.wait_recv()
            copies = [pltpu.make_async_copy(rtables.at[n], rtable.at[n], local_sem.at[n]) for n in range(row_count)]
            for copy in copies:
                copy.start()
            for copy in copies:
                copy.wait()

        def reached(behind, now):
            return jnp.clip(jnp.minimum(now - behind, 2 * (now - first_sums + 1)), 0, last)

        lax.fori_loop(reached(0, step - 1), reached(0, step), compute_line, 0)
        lax.fori_loop(reached(lag, step - 1), reached(lag, step), compute_cross, 0)
        return carry

    lax.fori_loop(0, last + lag + 1, advance, 0)

    def out_copy(part):
        some = pl.ds(part * piece, piece)
        return pltpu.make_async_copy(outs.at[some], out_ref.at[some], out_sem.at[part])

    def finish(part, carry):
        def one_row(j, carry):
            i = part * piece + j
            for w in range(2):
                outs[i, w] = (-0.5 * acc[i, :, w * LANES:(w + 1) * LANES]).astype(outs.dtype)
            return carry

        lax.fori_loop(0, piece, one_row, 0)
        out_copy(part).start()
        return carry

    lax.fori_loop(0, PARTS // 2, finish, 0)

    def close(part, carry):
        @pl.when(part < PARTS)
        def _():
            arrive(paired, cross, part)
            send(SIBLING, paired, cross, part, True)

        @pl.when(part > PARTS // 2)
        def _():
            compute(paired, part - 1, cross, cross_sibling)
            finish(part - 1, 0)

        return carry

    lax.fori_loop(PARTS // 2, PARTS + 1, close, 0)

    def drain(step, carry):
        @pl.when(step >= PARTS - WINDOW)
        def _():
            line_step(step, False)

        cross_step(step, False)
        return carry

    lax.fori_loop(0, last, drain, 0)
    for part in range(PARTS // 2, PARTS):
        extra(part, False)
        send(SIBLING, paired, cross, part, False)
    for n in range(1, row_count):
        for copy in row_copies(r, lax.rem(r + n, row_count)):
            copy.wait_send()
    for part in range(PARTS):
        out_copy(part).wait()


def shards(row_count, col_count, y_blocks, y_cols, prod_blocks, prod_cols, out_cols):
    rows, _, size, _ = y_blocks.shape
    table = jnp.concatenate([y_cols, y_cols % rows, prod_cols, out_cols[:, 0]], axis=1)
    table = jnp.pad(table, ((0, LANES - rows), (0, 3))).T
    anywhere = pl.BlockSpec(memory_space=pl.ANY)
    dma = pltpu.SemaphoreType.DMA
    y_next = pl.pallas_call(
        functools.partial(kernel, row_count, col_count),
        out_shape=jax.ShapeDtypeStruct((rows, 2, size, size), jnp.bfloat16),
        in_specs=[anywhere] * 3,
        out_specs=anywhere,
        scratch_shapes=[
            pltpu.VMEM((col_count, 4, rows, size, size), jnp.bfloat16),
            pltpu.VMEM((row_count * rows + 1, size, size), jnp.bfloat16),
            pltpu.VMEM((rows, size, 2 * size), jnp.float32),
            pltpu.VMEM((rows, 2, size, size), jnp.bfloat16),
            pltpu.VMEM((col_count, 4, 8, LANES), jnp.int32),
            pltpu.VMEM((row_count, 8, LANES), jnp.int32),
            pltpu.SMEM((col_count, 4, 8, LANES), jnp.int32),
            pltpu.SMEM((row_count + 1, 8, LANES), jnp.int32),
            dma((4, col_count, 4, PARTS)),
            dma((col_count, 4, PARTS)),
            dma((4, col_count, 4)),
            dma((col_count, 4)),
            dma((row_count,)),
            dma((row_count,)),
            dma((row_count,)),
            dma((row_count,)),
            dma((max(5, row_count),)),
            dma((PARTS,)),
        ],
        compiler_params=pltpu.CompilerParams(
            collective_id=0, has_side_effects=True, vmem_limit_bytes=56 * 1024 * 1024
        ),
    )(y_blocks.reshape(rows, size, size), prod_blocks.reshape(rows, size, size), table)
    return y_next.reshape(rows, 1, 2, size, size)


def solution(mesh):
    placed = (
        P("rows", ("cols", "layers"), None, None),
        P("rows", ("cols", "layers")),
        P("rows", ("cols", "layers"), None, None),
        P("rows", ("cols", "layers")),
        P("rows", ("cols", "layers"), None),
    )
    return jax.shard_map(
        functools.partial(shards, mesh.shape["rows"], mesh.shape["cols"]),
        mesh=mesh,
        in_specs=placed,
        out_specs=P("rows", ("cols", "layers"), None, None, None),
        check_vma=False,
    )
```

```python
import functools

import jax
import jax.numpy as jnp
from jax import lax
from jax.experimental import pallas as pl
from jax.experimental.pallas import tpu as pltpu
from jax.sharding import PartitionSpec as P

TILE_COLS = 6
LANES = 128
PARTS = 4
WINDOW = 4
TOGETHER = 2
MESH = pl.DeviceIdType.MESH
UP, DOWN, CROSS, SIBLING = range(4)


def kernel(
    row_count, col_count, y_ref, m_ref, table_ref, out_ref,
    yall, mall, acc, outs, ytables, rtables, ytable, rtable,
    send_sem, recv_sem, tsend_sem, trecv_sem, row_send, row_recv, rtable_send, rtable_recv, local_sem, out_sem,
):
    rows = y_ref.shape[0]
    piece = rows // PARTS
    r, z, l = lax.axis_index("rows"), lax.axis_index("cols"), lax.axis_index("layers")
    cross = lax.rem(l + 2, 4)
    sibling = l + 1 - 2 * lax.rem(l, 2)
    cross_sibling = lax.rem(sibling + 2, 4)
    paired = z + 1 - 2 * lax.rem(z, 2)
    targets = {UP: (r, z + 1, l), DOWN: (r, z - 1, l), CROSS: (r, z, cross), SIBLING: (r, z, sibling)}

    own_copies = [
        pltpu.make_async_copy(y_ref, yall.at[z, l], local_sem.at[0]),
        pltpu.make_async_copy(m_ref, mall.at[pl.ds(r * rows, rows)], local_sem.at[1]),
        pltpu.make_async_copy(table_ref, ytables.at[z, l], local_sem.at[2]),
        pltpu.make_async_copy(table_ref, rtables.at[r], local_sem.at[3]),
        pltpu.make_async_copy(table_ref, rtable.at[row_count], local_sem.at[4]),
    ]
    for copy in own_copies:
        copy.start()

    barrier = pltpu.get_barrier_semaphore()

    def greet(device):
        pl.semaphore_signal(barrier, inc=1, device_id=device, device_id_type=MESH)

    greet(targets[CROSS])
    greet(targets[SIBLING])
    for step in range(1, row_count):
        greet((lax.rem(r + step, row_count), z, l))

    @pl.when(z + 1 < col_count)
    def _():
        greet(targets[UP])

    @pl.when(z > 0)
    def _():
        greet(targets[DOWN])

    line_peers = jnp.where(z > 0, 1, 0) + jnp.where(z + 1 < col_count, 1, 0)
    pl.semaphore_wait(barrier, 1 + row_count + line_peers)

    for copy in own_copies:
        copy.wait()

    def chunk_copy(way, at, tile, part, device):
        return pltpu.make_async_remote_copy(
            src_ref=yall.at[at, tile, pl.ds(part * piece, piece)],
            dst_ref=yall.at[at, tile, pl.ds(part * piece, piece)],
            send_sem=send_sem.at[way, at, tile, part],
            recv_sem=recv_sem.at[at, tile, part],
            device_id=device,
            device_id_type=MESH,
        )

    def table_copy(way, at, tile, device):
        return pltpu.make_async_remote_copy(
            src_ref=ytables.at[at, tile],
            dst_ref=ytables.at[at, tile],
            send_sem=tsend_sem.at[way, at, tile],
            recv_sem=trecv_sem.at[at, tile],
            device_id=device,
            device_id_type=MESH,
        )

    def send(way, at, tile, part, start, device=None):
        device = targets[way] if device is None else device
        chunk = chunk_copy(way, at, tile, part, device)
        if start:
            chunk.start()
        else:
            chunk.wait_send()

        @pl.when(part == 0)
        def _():
            table = table_copy(way, at, tile, device)
            if start:
                table.start()
            else:
                table.wait_send()

    def arrive(at, tile, part):
        chunk_copy(SIBLING, at, tile, part, targets[SIBLING]).wait_recv()

        @pl.when(part == 0)
        def _():
            table_copy(SIBLING, at, tile, targets[SIBLING]).wait_recv()

    def origins(step):
        away, part = step // PARTS, lax.rem(step, PARTS)
        return away, part, ((z - away, z - away >= 0), (z + away, jnp.logical_and(z + away < col_count, away > 0)))

    def by_cross_link(at, part):
        return jnp.logical_not(jnp.logical_and(at == paired, part >= PARTS // 2))

    def line_step(step, start):
        away, part, sides = origins(step)
        for side, (at, valid) in enumerate(sides):
            @pl.when(valid)
            def _():
                if start:
                    @pl.when(away > 0)
                    def _():
                        arrive(at, l, part)

                if side == 0:
                    @pl.when(z + 1 < col_count)
                    def _():
                        send(UP, at, l, part, start)

                @pl.when(jnp.logical_and(z > 0, (away == 0) if side == 0 else True))
                def _():
                    send(DOWN, at, l, part, start)

                @pl.when(by_cross_link(at, part))
                def _():
                    send(CROSS, at, l, part, start)

                send(SIBLING, at, l, part, start)

    def cross_step(step, start):
        away, part, sides = origins(step)
        for at, valid in sides:
            @pl.when(jnp.logical_and(valid, by_cross_link(at, part)))
            def _():
                if start:
                    arrive(at, cross, part)
                send(SIBLING, at, cross, part, start)

    def compute(at, part, tiles, awaited):
        for tile in awaited:
            arrive(at, tile, part)

        @pl.when(part == 0)
        def _():
            copies = [
                pltpu.make_async_copy(ytables.at[at, tile], ytable.at[at, tile], local_sem.at[n])
                for n, tile in enumerate(tiles)
            ]
            for copy in copies:
                copy.start()
            for copy in copies:
                copy.wait()

        def some_rows(j, carry):
            sums = []
            for u in range(TOGETHER):
                i = part * piece + j * TOGETHER + u
                wanted = [rtable[row_count, 3, i], rtable[row_count, 4, i]]
                left, right = [], []
                for tile in tiles:
                    left.append(yall[at, tile, i])
                    first = TILE_COLS * (at * 4 + tile)
                    inner = ytable[at, tile, 0, i]
                    found = rtable[first // rows, 2, ytable[at, tile, 1, i]]
                    right.append(jnp.concatenate(
                        [mall[jnp.where(found == want, inner, row_count * rows)] for want in wanted], axis=1
                    ))
                sums.append(acc[i] + jnp.dot(
                    jnp.concatenate(left, axis=1), jnp.concatenate(right, axis=0),
                    preferred_element_type=jnp.float32,
                ))
            for u in range(TOGETHER):
                acc[part * piece + j * TOGETHER + u] = sums[u]
            return carry

        lax.fori_loop(0, piece // TOGETHER, some_rows, 0)

    def fused(at, away, part):
        return jnp.logical_and(by_cross_link(at, part), away <= 1)

    def compute_line(step, carry):
        away, part, sides = origins(step)
        for at, valid in sides:
            @pl.when(jnp.logical_and(valid, jnp.logical_not(fused(at, away, part))))
            def _():
                compute(at, part, (l, sibling), (sibling,))
        return carry

    def compute_cross(step, carry):
        away, part, sides = origins(step)
        for at, valid in sides:
            @pl.when(jnp.logical_and(valid, fused(at, away, part)))
            def _():
                compute(at, part, (l, sibling, cross, cross_sibling), (sibling, cross_sibling))

            @pl.when(jnp.logical_and(valid, jnp.logical_and(by_cross_link(at, part), away > 1)))
            def _():
                compute(at, part, (cross, cross_sibling), (cross_sibling,))
        return carry

    def row_copies(owner, other):
        device = (other, z, l)
        owned = pl.ds(owner * rows, rows)
        key = jnp.where(owner == r, other, owner)
        blocks = pltpu.make_async_remote_copy(
            src_ref=mall.at[owned],
            dst_ref=mall.at[owned],
            send_sem=row_send.at[key],
            recv_sem=row_recv.at[owner],
            device_id=device,
            device_id_type=MESH,
        )
        table = pltpu.make_async_remote_copy(
            src_ref=rtables.at[owner],
            dst_ref=rtables.at[owner],
            send_sem=rtable_send.at[key],
            recv_sem=rtable_recv.at[owner],
            device_id=device,
            device_id_type=MESH,
        )
        return blocks, table

    def extra(part, start):
        send(UP, z, cross, part, start, (r, paired, l))

    last = PARTS * col_count
    first_sums = last // 2
    lag = PARTS + 1

    def advance(step, carry):
        @pl.when(jnp.logical_and(step >= WINDOW, step < PARTS))
        def _():
            line_step(step - WINDOW, False)

        @pl.when(step < last)
        def _():
            line_step(step, True)

        @pl.when(step == 0)
        def _():
            for other in range(1, row_count):
                for copy in row_copies(r, lax.rem(r + other, row_count)):
                    copy.start()
            mall[row_count * rows] = jnp.zeros(mall.shape[1:], mall.dtype)

            def begin(i, carry):
                own = yall[z, l, i].astype(jnp.float32)
                for w in range(2):
                    scale = jnp.where(rtable[row_count, 3 + w, i] == rtable[row_count, 0, i], -3.0, 0.0)
                    acc[i, :, w * LANES:(w + 1) * LANES] = own * scale
                return carry

            lax.fori_loop(0, rows, begin, 0)

        @pl.when(step == last - 3)
        def _():
            for part in range(PARTS // 2, PARTS):
                extra(part, True)

        @pl.when(jnp.logical_and(step >= lag, step < last + lag))
        def _():
            cross_step(step - lag, True)

        @pl.when(step == first_sums)
        def _():
            for n in range(1, row_count):
                other = lax.rem(r + n, row_count)
                for copy in row_copies(other, other):
                    copy.wait_recv()
            copies = [pltpu.make_async_copy(rtables.at[n], rtable.at[n], local_sem.at[n]) for n in range(row_count)]
            for copy in copies:
                copy.start()
            for copy in copies:
                copy.wait()

        def reached(behind, now):
            return jnp.clip(jnp.minimum(now - behind, 2 * (now - first_sums + 1)), 0, last)

        lax.fori_loop(reached(0, step - 1), reached(0, step), compute_line, 0)
        lax.fori_loop(reached(lag, step - 1), reached(lag, step), compute_cross, 0)
        return carry

    lax.fori_loop(0, last + lag + 1, advance, 0)

    def out_copy(part):
        some = pl.ds(part * piece, piece)
        return pltpu.make_async_copy(outs.at[some], out_ref.at[some], out_sem.at[part])

    def finish(part, carry):
        def one_row(j, carry):
            i = part * piece + j
            for w in range(2):
                outs[i, w] = (-0.5 * acc[i, :, w * LANES:(w + 1) * LANES]).astype(outs.dtype)
            return carry

        lax.fori_loop(0, piece, one_row, 0)
        out_copy(part).start()
        return carry

    lax.fori_loop(0, PARTS // 2, finish, 0)

    def close(part, carry):
        @pl.when(part < PARTS)
        def _():
            arrive(paired, cross, part)
            send(SIBLING, paired, cross, part, True)

        @pl.when(part > PARTS // 2)
        def _():
            compute(paired, part - 1, (cross, cross_sibling), (cross_sibling,))
            finish(part - 1, 0)

        return carry

    lax.fori_loop(PARTS // 2, PARTS + 1, close, 0)

    def drain(step, carry):
        @pl.when(step >= PARTS - WINDOW)
        def _():
            line_step(step, False)

        cross_step(step, False)
        return carry

    lax.fori_loop(0, last, drain, 0)
    for part in range(PARTS // 2, PARTS):
        extra(part, False)
        send(SIBLING, paired, cross, part, False)
    for n in range(1, row_count):
        for copy in row_copies(r, lax.rem(r + n, row_count)):
            copy.wait_send()
    for part in range(PARTS):
        out_copy(part).wait()


def shards(row_count, col_count, y_blocks, y_cols, prod_blocks, prod_cols, out_cols):
    rows, _, size, _ = y_blocks.shape
    table = jnp.concatenate([y_cols, y_cols % rows, prod_cols, out_cols[:, 0]], axis=1)
    table = jnp.pad(table, ((0, LANES - rows), (0, 3))).T
    anywhere = pl.BlockSpec(memory_space=pl.ANY)
    dma = pltpu.SemaphoreType.DMA
    y_next = pl.pallas_call(
        functools.partial(kernel, row_count, col_count),
        out_shape=jax.ShapeDtypeStruct((rows, 2, size, size), jnp.bfloat16),
        in_specs=[anywhere] * 3,
        out_specs=anywhere,
        scratch_shapes=[
            pltpu.VMEM((col_count, 4, rows, size, size), jnp.bfloat16),
            pltpu.VMEM((row_count * rows + 1, size, size), jnp.bfloat16),
            pltpu.VMEM((rows, size, 2 * size), jnp.float32),
            pltpu.VMEM((rows, 2, size, size), jnp.bfloat16),
            pltpu.VMEM((col_count, 4, 8, LANES), jnp.int32),
            pltpu.VMEM((row_count, 8, LANES), jnp.int32),
            pltpu.SMEM((col_count, 4, 8, LANES), jnp.int32),
            pltpu.SMEM((row_count + 1, 8, LANES), jnp.int32),
            dma((4, col_count, 4, PARTS)),
            dma((col_count, 4, PARTS)),
            dma((4, col_count, 4)),
            dma((col_count, 4)),
            dma((row_count,)),
            dma((row_count,)),
            dma((row_count,)),
            dma((row_count,)),
            dma((max(5, row_count),)),
            dma((PARTS,)),
        ],
        compiler_params=pltpu.CompilerParams(
            collective_id=0, has_side_effects=True, vmem_limit_bytes=56 * 1024 * 1024
        ),
    )(y_blocks.reshape(rows, size, size), prod_blocks.reshape(rows, size, size), table)
    return y_next.reshape(rows, 1, 2, size, size)


def solution(mesh):
    placed = (
        P("rows", ("cols", "layers"), None, None),
        P("rows", ("cols", "layers")),
        P("rows", ("cols", "layers"), None, None),
        P("rows", ("cols", "layers")),
        P("rows", ("cols", "layers"), None),
    )
    return jax.shard_map(
        functools.partial(shards, mesh.shape["rows"], mesh.shape["cols"]),
        mesh=mesh,
        in_specs=placed,
        out_specs=P("rows", ("cols", "layers"), None, None, None),
        check_vma=False,
    )
```

```python
import functools

import jax
import jax.numpy as jnp
from jax import lax
from jax.experimental import pallas as pl
from jax.experimental.pallas import tpu as pltpu
from jax.sharding import PartitionSpec as P

TILE_COLS = 6
LANES = 128
PARTS = 4
TOGETHER = 2
MESH = pl.DeviceIdType.MESH
UP, DOWN, CROSS, SIBLING = range(4)


def kernel(
    row_count, col_count, y_ref, m_ref, table_ref, out_ref,
    yall, mall, acc, outs, ytables, rtables, ytable, rtable,
    send_sem, recv_sem, tsend_sem, trecv_sem, row_send, row_recv, rtable_send, rtable_recv, local_sem, out_sem,
):
    rows = y_ref.shape[0]
    piece = rows // PARTS
    r, z, l = lax.axis_index("rows"), lax.axis_index("cols"), lax.axis_index("layers")
    cross = lax.rem(l + 2, 4)
    sibling = l + 1 - 2 * lax.rem(l, 2)
    cross_sibling = lax.rem(sibling + 2, 4)
    paired = z + 1 - 2 * lax.rem(z, 2)
    targets = {UP: (r, z + 1, l), DOWN: (r, z - 1, l), CROSS: (r, z, cross), SIBLING: (r, z, sibling)}

    own_copies = [
        pltpu.make_async_copy(y_ref, yall.at[z, l], local_sem.at[0]),
        pltpu.make_async_copy(m_ref, mall.at[pl.ds(r * rows, rows)], local_sem.at[1]),
        pltpu.make_async_copy(table_ref, ytables.at[z, l], local_sem.at[2]),
        pltpu.make_async_copy(table_ref, rtables.at[r], local_sem.at[3]),
        pltpu.make_async_copy(table_ref, rtable.at[row_count], local_sem.at[4]),
    ]
    for copy in own_copies:
        copy.start()

    barrier = pltpu.get_barrier_semaphore()

    def greet(device):
        pl.semaphore_signal(barrier, inc=1, device_id=device, device_id_type=MESH)

    greet(targets[CROSS])
    greet(targets[SIBLING])
    for step in range(1, row_count):
        greet((lax.rem(r + step, row_count), z, l))

    @pl.when(z + 1 < col_count)
    def _():
        greet(targets[UP])

    @pl.when(z > 0)
    def _():
        greet(targets[DOWN])

    line_peers = jnp.where(z > 0, 1, 0) + jnp.where(z + 1 < col_count, 1, 0)
    pl.semaphore_wait(barrier, 1 + row_count + line_peers)

    for copy in own_copies:
        copy.wait()

    def chunk_copy(way, at, tile, part, device):
        return pltpu.make_async_remote_copy(
            src_ref=yall.at[at, tile, pl.ds(part * piece, piece)],
            dst_ref=yall.at[at, tile, pl.ds(part * piece, piece)],
            send_sem=send_sem.at[way, at, tile, part],
            recv_sem=recv_sem.at[at, tile, part],
            device_id=device,
            device_id_type=MESH,
        )

    def table_copy(way, at, tile, device):
        return pltpu.make_async_remote_copy(
            src_ref=ytables.at[at, tile],
            dst_ref=ytables.at[at, tile],
            send_sem=tsend_sem.at[way, at, tile],
            recv_sem=trecv_sem.at[at, tile],
            device_id=device,
            device_id_type=MESH,
        )

    def send(way, at, tile, part, start, device=None):
        device = targets[way] if device is None else device
        chunk = chunk_copy(way, at, tile, part, device)
        if start:
            chunk.start()
        else:
            chunk.wait_send()

        @pl.when(part == 0)
        def _():
            table = table_copy(way, at, tile, device)
            if start:
                table.start()
            else:
                table.wait_send()

    def arrive(at, tile, part):
        chunk_copy(SIBLING, at, tile, part, targets[SIBLING]).wait_recv()

        @pl.when(part == 0)
        def _():
            table_copy(SIBLING, at, tile, targets[SIBLING]).wait_recv()

    def origins(step):
        away, part = step // PARTS, lax.rem(step, PARTS)
        return away, part, ((z - away, z - away >= 0), (z + away, jnp.logical_and(z + away < col_count, away > 0)))

    def by_cross_link(at, part):
        return jnp.logical_not(jnp.logical_and(at == paired, part >= PARTS // 2))

    def line_step(step, start):
        away, part, sides = origins(step)
        for side, (at, valid) in enumerate(sides):
            @pl.when(valid)
            def _():
                if start:
                    @pl.when(away > 0)
                    def _():
                        arrive(at, l, part)

                if side == 0:
                    @pl.when(z + 1 < col_count)
                    def _():
                        send(UP, at, l, part, start)

                @pl.when(jnp.logical_and(z > 0, (away == 0) if side == 0 else True))
                def _():
                    send(DOWN, at, l, part, start)

                @pl.when(by_cross_link(at, part))
                def _():
                    send(CROSS, at, l, part, start)

                send(SIBLING, at, l, part, start)

    def cross_step(step, start):
        away, part, sides = origins(step)
        for at, valid in sides:
            @pl.when(jnp.logical_and(valid, by_cross_link(at, part)))
            def _():
                if start:
                    arrive(at, cross, part)
                send(SIBLING, at, cross, part, start)

    def compute(at, part, tiles, awaited):
        for tile in awaited:
            arrive(at, tile, part)

        @pl.when(part == 0)
        def _():
            copies = [
                pltpu.make_async_copy(ytables.at[at, tile], ytable.at[at, tile], local_sem.at[n])
                for n, tile in enumerate(tiles)
            ]
            for copy in copies:
                copy.start()
            for copy in copies:
                copy.wait()

        def some_rows(j, carry):
            sums = []
            for u in range(TOGETHER):
                i = part * piece + j * TOGETHER + u
                wanted = [rtable[row_count, 3, i], rtable[row_count, 4, i]]
                left, right = [], []
                for tile in tiles:
                    left.append(yall[at, tile, i])
                    first = TILE_COLS * (at * 4 + tile)
                    inner = ytable[at, tile, 0, i]
                    found = rtable[first // rows, 2, ytable[at, tile, 1, i]]
                    right.append(jnp.concatenate(
                        [mall[jnp.where(found == want, inner, row_count * rows)] for want in wanted], axis=1
                    ))
                sums.append(acc[i] + jnp.dot(
                    jnp.concatenate(left, axis=1), jnp.concatenate(right, axis=0),
                    preferred_element_type=jnp.float32,
                ))
            for u in range(TOGETHER):
                acc[part * piece + j * TOGETHER + u] = sums[u]
            return carry

        lax.fori_loop(0, piece // TOGETHER, some_rows, 0)

    def fused(at, away, part):
        return jnp.logical_and(by_cross_link(at, part), away <= 1)

    def compute_line(step, carry):
        away, part, sides = origins(step)
        for at, valid in sides:
            @pl.when(jnp.logical_and(valid, jnp.logical_not(fused(at, away, part))))
            def _():
                compute(at, part, (l, sibling), (sibling,))
        return carry

    def compute_cross(step, carry):
        away, part, sides = origins(step)
        for at, valid in sides:
            @pl.when(jnp.logical_and(valid, fused(at, away, part)))
            def _():
                compute(at, part, (l, sibling, cross, cross_sibling), (sibling, cross_sibling))

            @pl.when(jnp.logical_and(valid, jnp.logical_and(by_cross_link(at, part), away > 1)))
            def _():
                compute(at, part, (cross, cross_sibling), (cross_sibling,))
        return carry

    def row_copies(owner, other):
        device = (other, z, l)
        owned = pl.ds(owner * rows, rows)
        key = jnp.where(owner == r, other, owner)
        blocks = pltpu.make_async_remote_copy(
            src_ref=mall.at[owned],
            dst_ref=mall.at[owned],
            send_sem=row_send.at[key],
            recv_sem=row_recv.at[owner],
            device_id=device,
            device_id_type=MESH,
        )
        table = pltpu.make_async_remote_copy(
            src_ref=rtables.at[owner],
            dst_ref=rtables.at[owner],
            send_sem=rtable_send.at[key],
            recv_sem=rtable_recv.at[owner],
            device_id=device,
            device_id_type=MESH,
        )
        return blocks, table

    def extra(part, start):
        send(UP, z, cross, part, start, (r, paired, l))

    last = PARTS * col_count
    first_sums = last // 2
    lag = PARTS + 1

    def advance(step, carry):
        @pl.when(step < last)
        def _():
            line_step(step, True)

        @pl.when(step == 0)
        def _():
            for other in range(1, row_count):
                for copy in row_copies(r, lax.rem(r + other, row_count)):
                    copy.start()
            mall[row_count * rows] = jnp.zeros(mall.shape[1:], mall.dtype)

            def begin(i, carry):
                own = yall[z, l, i].astype(jnp.float32)
                for w in range(2):
                    scale = jnp.where(rtable[row_count, 3 + w, i] == rtable[row_count, 0, i], -3.0, 0.0)
                    acc[i, :, w * LANES:(w + 1) * LANES] = own * scale
                return carry

            lax.fori_loop(0, rows, begin, 0)

        @pl.when(step == last - 3)
        def _():
            for part in range(PARTS // 2, PARTS):
                extra(part, True)

        @pl.when(jnp.logical_and(step >= lag, step < last + lag))
        def _():
            cross_step(step - lag, True)

        @pl.when(step == first_sums)
        def _():
            for n in range(1, row_count):
                other = lax.rem(r + n, row_count)
                for copy in row_copies(other, other):
                    copy.wait_recv()
            copies = [pltpu.make_async_copy(rtables.at[n], rtable.at[n], local_sem.at[n]) for n in range(row_count)]
            for copy in copies:
                copy.start()
            for copy in copies:
                copy.wait()

        def reached(behind, now):
            return jnp.clip(jnp.minimum(now - behind, 2 * (now - first_sums + 1)), 0, last)

        lax.fori_loop(reached(0, step - 1), reached(0, step), compute_line, 0)
        lax.fori_loop(reached(lag, step - 1), reached(lag, step), compute_cross, 0)

        @pl.when(jnp.logical_and(step >= 2 * PARTS, step < last + 2 * PARTS))
        def _():
            line_step(step - 2 * PARTS, False)

        @pl.when(step >= lag + PARTS)
        def _():
            cross_step(step - lag - PARTS, False)

        return carry

    lax.fori_loop(0, last + lag + 1, advance, 0)

    def out_copy(part):
        some = pl.ds(part * piece, piece)
        return pltpu.make_async_copy(outs.at[some], out_ref.at[some], out_sem.at[part])

    def finish(part, carry):
        def one_row(j, carry):
            i = part * piece + j
            for w in range(2):
                outs[i, w] = (-0.5 * acc[i, :, w * LANES:(w + 1) * LANES]).astype(outs.dtype)
            return carry

        lax.fori_loop(0, piece, one_row, 0)
        out_copy(part).start()
        return carry

    lax.fori_loop(0, PARTS // 2, finish, 0)

    def close(part, carry):
        @pl.when(part < PARTS)
        def _():
            arrive(paired, cross, part)
            send(SIBLING, paired, cross, part, True)

        @pl.when(part > PARTS // 2)
        def _():
            compute(paired, part - 1, (cross, cross_sibling), (cross_sibling,))
            finish(part - 1, 0)

        return carry

    lax.fori_loop(PARTS // 2, PARTS + 1, close, 0)

    def drain(step, carry):
        @pl.when(step >= last + lag + 1 - 2 * PARTS)
        def _():
            line_step(step, False)

        @pl.when(step >= last + 1 - PARTS)
        def _():
            cross_step(step, False)

        return carry

    lax.fori_loop(last + 1 - 2 * PARTS, last, drain, 0)
    for part in range(PARTS // 2, PARTS):
        extra(part, False)
        send(SIBLING, paired, cross, part, False)
    for n in range(1, row_count):
        for copy in row_copies(r, lax.rem(r + n, row_count)):
            copy.wait_send()
    for part in range(PARTS):
        out_copy(part).wait()


def shards(row_count, col_count, y_blocks, y_cols, prod_blocks, prod_cols, out_cols):
    rows, _, size, _ = y_blocks.shape
    table = jnp.concatenate([y_cols, y_cols % rows, prod_cols, out_cols[:, 0]], axis=1)
    table = jnp.pad(table, ((0, LANES - rows), (0, 3))).T
    anywhere = pl.BlockSpec(memory_space=pl.ANY)
    dma = pltpu.SemaphoreType.DMA
    y_next = pl.pallas_call(
        functools.partial(kernel, row_count, col_count),
        out_shape=jax.ShapeDtypeStruct((rows, 2, size, size), jnp.bfloat16),
        in_specs=[anywhere] * 3,
        out_specs=anywhere,
        scratch_shapes=[
            pltpu.VMEM((col_count, 4, rows, size, size), jnp.bfloat16),
            pltpu.VMEM((row_count * rows + 1, size, size), jnp.bfloat16),
            pltpu.VMEM((rows, size, 2 * size), jnp.float32),
            pltpu.VMEM((rows, 2, size, size), jnp.bfloat16),
            pltpu.VMEM((col_count, 4, 8, LANES), jnp.int32),
            pltpu.VMEM((row_count, 8, LANES), jnp.int32),
            pltpu.SMEM((col_count, 4, 8, LANES), jnp.int32),
            pltpu.SMEM((row_count + 1, 8, LANES), jnp.int32),
            dma((4, col_count, 4, PARTS)),
            dma((col_count, 4, PARTS)),
            dma((4, col_count, 4)),
            dma((col_count, 4)),
            dma((row_count,)),
            dma((row_count,)),
            dma((row_count,)),
            dma((row_count,)),
            dma((max(5, row_count),)),
            dma((PARTS,)),
        ],
        compiler_params=pltpu.CompilerParams(
            collective_id=0, has_side_effects=True, vmem_limit_bytes=56 * 1024 * 1024
        ),
    )(y_blocks.reshape(rows, size, size), prod_blocks.reshape(rows, size, size), table)
    return y_next.reshape(rows, 1, 2, size, size)


def solution(mesh):
    placed = (
        P("rows", ("cols", "layers"), None, None),
        P("rows", ("cols", "layers")),
        P("rows", ("cols", "layers"), None, None),
        P("rows", ("cols", "layers")),
        P("rows", ("cols", "layers"), None),
    )
    return jax.shard_map(
        functools.partial(shards, mesh.shape["rows"], mesh.shape["cols"]),
        mesh=mesh,
        in_specs=placed,
        out_specs=P("rows", ("cols", "layers"), None, None, None),
        check_vma=False,
    )
```

```python
import functools

import jax
import jax.numpy as jnp
from jax import lax
from jax.experimental import pallas as pl
from jax.experimental.pallas import tpu as pltpu
from jax.sharding import PartitionSpec as P

TILE_COLS = 6
LANES = 128
PARTS = 4
BY_LINE_FROM = 1
TOGETHER = 2
MESH = pl.DeviceIdType.MESH
UP, DOWN, CROSS, SIBLING = range(4)


def kernel(
    row_count, col_count, y_ref, m_ref, table_ref, out_ref,
    yall, mall, acc, outs, ytables, rtables, ytable, rtable,
    send_sem, recv_sem, tsend_sem, trecv_sem, row_send, row_recv, rtable_send, rtable_recv, local_sem, out_sem,
):
    rows = y_ref.shape[0]
    piece = rows // PARTS
    r, z, l = lax.axis_index("rows"), lax.axis_index("cols"), lax.axis_index("layers")
    cross = lax.rem(l + 2, 4)
    sibling = l + 1 - 2 * lax.rem(l, 2)
    cross_sibling = lax.rem(sibling + 2, 4)
    paired = z + 1 - 2 * lax.rem(z, 2)
    targets = {UP: (r, z + 1, l), DOWN: (r, z - 1, l), CROSS: (r, z, cross), SIBLING: (r, z, sibling)}

    own_copies = [
        pltpu.make_async_copy(y_ref, yall.at[z, l], local_sem.at[0]),
        pltpu.make_async_copy(m_ref, mall.at[pl.ds(r * rows, rows)], local_sem.at[1]),
        pltpu.make_async_copy(table_ref, ytables.at[z, l], local_sem.at[2]),
        pltpu.make_async_copy(table_ref, rtables.at[r], local_sem.at[3]),
        pltpu.make_async_copy(table_ref, rtable.at[row_count], local_sem.at[4]),
    ]
    for copy in own_copies:
        copy.start()

    barrier = pltpu.get_barrier_semaphore()

    def greet(device):
        pl.semaphore_signal(barrier, inc=1, device_id=device, device_id_type=MESH)

    greet(targets[CROSS])
    greet(targets[SIBLING])
    for step in range(1, row_count):
        greet((lax.rem(r + step, row_count), z, l))

    @pl.when(z + 1 < col_count)
    def _():
        greet(targets[UP])

    @pl.when(z > 0)
    def _():
        greet(targets[DOWN])

    line_peers = jnp.where(z > 0, 1, 0) + jnp.where(z + 1 < col_count, 1, 0)
    pl.semaphore_wait(barrier, 1 + row_count + line_peers)

    for copy in own_copies:
        copy.wait()

    def chunk_copy(way, at, tile, part, device):
        return pltpu.make_async_remote_copy(
            src_ref=yall.at[at, tile, pl.ds(part * piece, piece)],
            dst_ref=yall.at[at, tile, pl.ds(part * piece, piece)],
            send_sem=send_sem.at[way, at, tile, part],
            recv_sem=recv_sem.at[at, tile, part],
            device_id=device,
            device_id_type=MESH,
        )

    def table_copy(way, at, tile, device):
        return pltpu.make_async_remote_copy(
            src_ref=ytables.at[at, tile],
            dst_ref=ytables.at[at, tile],
            send_sem=tsend_sem.at[way, at, tile],
            recv_sem=trecv_sem.at[at, tile],
            device_id=device,
            device_id_type=MESH,
        )

    def send(way, at, tile, part, start, device=None):
        device = targets[way] if device is None else device
        chunk = chunk_copy(way, at, tile, part, device)
        if start:
            chunk.start()
        else:
            chunk.wait_send()

        @pl.when(part == 0)
        def _():
            table = table_copy(way, at, tile, device)
            if start:
                table.start()
            else:
                table.wait_send()

    def arrive(at, tile, part):
        chunk_copy(SIBLING, at, tile, part, targets[SIBLING]).wait_recv()

        @pl.when(part == 0)
        def _():
            table_copy(SIBLING, at, tile, targets[SIBLING]).wait_recv()

    def origins(step):
        away, part = step // PARTS, lax.rem(step, PARTS)
        return away, part, ((z - away, z - away >= 0), (z + away, jnp.logical_and(z + away < col_count, away > 0)))

    def by_cross_link(at, part):
        return jnp.logical_not(jnp.logical_and(at == paired, part >= BY_LINE_FROM))

    def line_step(step, start):
        away, part, sides = origins(step)
        for side, (at, valid) in enumerate(sides):
            @pl.when(valid)
            def _():
                if start:
                    @pl.when(away > 0)
                    def _():
                        arrive(at, l, part)

                if side == 0:
                    @pl.when(z + 1 < col_count)
                    def _():
                        send(UP, at, l, part, start)

                @pl.when(jnp.logical_and(z > 0, (away == 0) if side == 0 else True))
                def _():
                    send(DOWN, at, l, part, start)

                @pl.when(by_cross_link(at, part))
                def _():
                    send(CROSS, at, l, part, start)

                send(SIBLING, at, l, part, start)

    def cross_step(step, start):
        away, part, sides = origins(step)
        for at, valid in sides:
            @pl.when(jnp.logical_and(valid, by_cross_link(at, part)))
            def _():
                if start:
                    arrive(at, cross, part)
                send(SIBLING, at, cross, part, start)

    def compute(at, part, tiles, awaited):
        for tile in awaited:
            arrive(at, tile, part)

        @pl.when(part == 0)
        def _():
            copies = [
                pltpu.make_async_copy(ytables.at[at, tile], ytable.at[at, tile], local_sem.at[n])
                for n, tile in enumerate(tiles)
            ]
            for copy in copies:
                copy.start()
            for copy in copies:
                copy.wait()

        def some_rows(j, carry):
            sums = []
            for u in range(TOGETHER):
                i = part * piece + j * TOGETHER + u
                wanted = [rtable[row_count, 3, i], rtable[row_count, 4, i]]
                left, right = [], []
                for tile in tiles:
                    left.append(yall[at, tile, i])
                    first = TILE_COLS * (at * 4 + tile)
                    inner = ytable[at, tile, 0, i]
                    found = rtable[first // rows, 2, ytable[at, tile, 1, i]]
                    right.append(jnp.concatenate(
                        [mall[jnp.where(found == want, inner, row_count * rows)] for want in wanted], axis=1
                    ))
                sums.append(acc[i] + jnp.dot(
                    jnp.concatenate(left, axis=1), jnp.concatenate(right, axis=0),
                    preferred_element_type=jnp.float32,
                ))
            for u in range(TOGETHER):
                acc[part * piece + j * TOGETHER + u] = sums[u]
            return carry

        lax.fori_loop(0, piece // TOGETHER, some_rows, 0)

    def fused(at, away, part):
        return jnp.logical_and(by_cross_link(at, part), away == 0)

    def compute_line(step, carry):
        away, part, sides = origins(step)
        for at, valid in sides:
            @pl.when(jnp.logical_and(valid, jnp.logical_not(fused(at, away, part))))
            def _():
                compute(at, part, (l, sibling), (sibling,))
        return carry

    def compute_cross(step, carry):
        away, part, sides = origins(step)
        for at, valid in sides:
            @pl.when(jnp.logical_and(valid, fused(at, away, part)))
            def _():
                compute(at, part, (l, sibling, cross, cross_sibling), (sibling, cross_sibling))

            @pl.when(jnp.logical_and(valid, jnp.logical_and(by_cross_link(at, part), away > 0)))
            def _():
                compute(at, part, (cross, cross_sibling), (cross_sibling,))
        return carry

    def row_copies(owner, other):
        device = (other, z, l)
        owned = pl.ds(owner * rows, rows)
        key = jnp.where(owner == r, other, owner)
        blocks = pltpu.make_async_remote_copy(
            src_ref=mall.at[owned],
            dst_ref=mall.at[owned],
            send_sem=row_send.at[key],
            recv_sem=row_recv.at[owner],
            device_id=device,
            device_id_type=MESH,
        )
        table = pltpu.make_async_remote_copy(
            src_ref=rtables.at[owner],
            dst_ref=rtables.at[owner],
            send_sem=rtable_send.at[key],
            recv_sem=rtable_recv.at[owner],
            device_id=device,
            device_id_type=MESH,
        )
        return blocks, table

    def extra(part, start):
        send(UP, z, cross, part, start, (r, paired, l))

    last = PARTS * col_count
    first_sums = last // 2
    lag = PARTS + 1

    def advance(step, carry):
        @pl.when(step < last)
        def _():
            line_step(step, True)

        @pl.when(step == 0)
        def _():
            for other in range(1, row_count):
                for copy in row_copies(r, lax.rem(r + other, row_count)):
                    copy.start()
            mall[row_count * rows] = jnp.zeros(mall.shape[1:], mall.dtype)

            def begin(i, carry):
                own = yall[z, l, i].astype(jnp.float32)
                for w in range(2):
                    scale = jnp.where(rtable[row_count, 3 + w, i] == rtable[row_count, 0, i], -3.0, 0.0)
                    acc[i, :, w * LANES:(w + 1) * LANES] = own * scale
                return carry

            lax.fori_loop(0, rows, begin, 0)

        @pl.when(step == last - 3)
        def _():
            for part in range(BY_LINE_FROM, PARTS):
                extra(part, True)

        @pl.when(jnp.logical_and(step >= lag, step < last + lag))
        def _():
            cross_step(step - lag, True)

        @pl.when(step == first_sums)
        def _():
            for n in range(1, row_count):
                other = lax.rem(r + n, row_count)
                for copy in row_copies(other, other):
                    copy.wait_recv()
            copies = [pltpu.make_async_copy(rtables.at[n], rtable.at[n], local_sem.at[n]) for n in range(row_count)]
            for copy in copies:
                copy.start()
            for copy in copies:
                copy.wait()

        def reached(behind, now):
            return jnp.clip(jnp.minimum(now - behind, 2 * (now - first_sums + 1)), 0, last)

        lax.fori_loop(reached(0, step - 1), reached(0, step), compute_line, 0)
        lax.fori_loop(reached(lag, step - 1), reached(lag, step), compute_cross, 0)

        @pl.when(jnp.logical_and(step >= 2 * PARTS, step < last + 2 * PARTS))
        def _():
            line_step(step - 2 * PARTS, False)

        @pl.when(step >= lag + PARTS)
        def _():
            cross_step(step - lag - PARTS, False)

        return carry

    lax.fori_loop(0, last + lag + 1, advance, 0)

    def out_copy(part):
        some = pl.ds(part * piece, piece)
        return pltpu.make_async_copy(outs.at[some], out_ref.at[some], out_sem.at[part])

    def finish(part, carry):
        def one_row(j, carry):
            i = part * piece + j
            for w in range(2):
                outs[i, w] = (-0.5 * acc[i, :, w * LANES:(w + 1) * LANES]).astype(outs.dtype)
            return carry

        lax.fori_loop(0, piece, one_row, 0)
        out_copy(part).start()
        return carry

    lax.fori_loop(0, BY_LINE_FROM, finish, 0)

    def close(part, carry):
        @pl.when(part < PARTS)
        def _():
            arrive(paired, cross, part)
            send(SIBLING, paired, cross, part, True)

        @pl.when(part > BY_LINE_FROM)
        def _():
            compute(paired, part - 1, (cross, cross_sibling), (cross_sibling,))
            finish(part - 1, 0)

        return carry

    lax.fori_loop(BY_LINE_FROM, PARTS + 1, close, 0)

    def drain(step, carry):
        @pl.when(step >= last + lag + 1 - 2 * PARTS)
        def _():
            line_step(step, False)

        @pl.when(step >= last + 1 - PARTS)
        def _():
            cross_step(step, False)

        return carry

    lax.fori_loop(last + 1 - 2 * PARTS, last, drain, 0)
    for part in range(BY_LINE_FROM, PARTS):
        extra(part, False)
        send(SIBLING, paired, cross, part, False)
    for n in range(1, row_count):
        for copy in row_copies(r, lax.rem(r + n, row_count)):
            copy.wait_send()
    for part in range(PARTS):
        out_copy(part).wait()


def shards(row_count, col_count, y_blocks, y_cols, prod_blocks, prod_cols, out_cols):
    rows, _, size, _ = y_blocks.shape
    table = jnp.concatenate([y_cols, y_cols % rows, prod_cols, out_cols[:, 0]], axis=1)
    table = jnp.pad(table, ((0, LANES - rows), (0, 3))).T
    anywhere = pl.BlockSpec(memory_space=pl.ANY)
    dma = pltpu.SemaphoreType.DMA
    y_next = pl.pallas_call(
        functools.partial(kernel, row_count, col_count),
        out_shape=jax.ShapeDtypeStruct((rows, 2, size, size), jnp.bfloat16),
        in_specs=[anywhere] * 3,
        out_specs=anywhere,
        scratch_shapes=[
            pltpu.VMEM((col_count, 4, rows, size, size), jnp.bfloat16),
            pltpu.VMEM((row_count * rows + 1, size, size), jnp.bfloat16),
            pltpu.VMEM((rows, size, 2 * size), jnp.float32),
            pltpu.VMEM((rows, 2, size, size), jnp.bfloat16),
            pltpu.VMEM((col_count, 4, 8, LANES), jnp.int32),
            pltpu.VMEM((row_count, 8, LANES), jnp.int32),
            pltpu.SMEM((col_count, 4, 8, LANES), jnp.int32),
            pltpu.SMEM((row_count + 1, 8, LANES), jnp.int32),
            dma((4, col_count, 4, PARTS)),
            dma((col_count, 4, PARTS)),
            dma((4, col_count, 4)),
            dma((col_count, 4)),
            dma((row_count,)),
            dma((row_count,)),
            dma((row_count,)),
            dma((row_count,)),
            dma((max(5, row_count),)),
            dma((PARTS,)),
        ],
        compiler_params=pltpu.CompilerParams(
            collective_id=0, has_side_effects=True, vmem_limit_bytes=56 * 1024 * 1024
        ),
    )(y_blocks.reshape(rows, size, size), prod_blocks.reshape(rows, size, size), table)
    return y_next.reshape(rows, 1, 2, size, size)


def solution(mesh):
    placed = (
        P("rows", ("cols", "layers"), None, None),
        P("rows", ("cols", "layers")),
        P("rows", ("cols", "layers"), None, None),
        P("rows", ("cols", "layers")),
        P("rows", ("cols", "layers"), None),
    )
    return jax.shard_map(
        functools.partial(shards, mesh.shape["rows"], mesh.shape["cols"]),
        mesh=mesh,
        in_specs=placed,
        out_specs=P("rows", ("cols", "layers"), None, None, None),
        check_vma=False,
    )
```
